32 devices in a mesh: grp: 2 (over x), band: 16 (over z, y, core).
Axes of the slice: x: 2, y: 2, z: 4, core: 2. Of those that a mesh axis runs over, the one named last changes fastest.
Arguments:
- opacity_deriv: bfloat16 [4, 1024, 4096], P('grp', None, 'band'), parts along dimension 0, may hold values from -6 to 6
- emission_deriv: bfloat16 [4, 1024, 4096], P('grp', None, 'band'), parts along dimension 0, may hold values from -0.09375 to 0.09375
- kernel_tiles: float32 [8, 128, 128], replicated, may hold values from 0.1 to 1
- tile_map: int32 [4, 8, 8], P('grp'), parts along dimension 0, may hold values from 0 to 7
- active_counts: int32 [4], P('grp'), parts along dimension 0, may hold values from 512 to 1024, as said below
Outputs:
- jacobian: float32 [1024, 4, 1024], P('band', 'grp'), parts along dimension 1
The draws below stay inside these ranges and needn't reach their ends.
There are 2 independent parts, one for each index of `grp`. The reference program is written for one: setup_inputs(seed, part) draws one part's arguments, and reference() takes and returns one part's arrays. A program takes and returns all parts, laid end to end along the dimension named above; an argument that names none is the same for every part. Nothing has to cross between parts.
Inputs may be any that keep to these rules, and one draw needn't show every extreme that they name: `active_counts`: at least one line of each batch has all 1024 cells active.
All inputs are finite; a program needn't handle non-finite values.
Results may differ from the reference program's by a relative error of at most 0.0003.
Values may be sent and summed in bfloat16 or wider, within the bound.
A program may use at most 64 MiB of HBM per device.

```python
import jax
import jax.numpy as jnp

LINES = 2
CELLS = 1024
BANDS = 4096
TILE = 128
KINDS = 8
BLOCKS = 8


def draw_active_counts(key, part):
    values = jax.random.randint(key, (LINES,), CELLS // 2, CELLS + 1, dtype=jnp.int32)
    full_line = jax.random.randint(jax.random.fold_in(key, 7), (), 0, LINES, dtype=jnp.int32)
    positions = jnp.arange(LINES, dtype=jnp.int32)
    return jnp.where(positions == full_line, jnp.int32(CELLS), values)


def set_ends(drawn, own_key, smallest, top_value):
    shape = drawn.shape
    spot = [jax.random.randint(jax.random.fold_in(own_key, axis), (), 0, shape[axis]) for axis in range(len(shape))]
    drawn = drawn.at[tuple(spot)].set(smallest)
    longest = shape.index(max(shape))
    spot[longest] = (spot[longest] + 1) % shape[longest]
    return drawn.at[tuple(spot)].set(top_value)


def spiked(drawn, key, source, target, blocks, factor):
    owner, partner = [(jnp.arange(drawn.shape[position]) // (drawn.shape[position] // blocks)).reshape([-1 if axis == position else 1 for axis in range(drawn.ndim)]) for position in (source, target)]
    chosen = jax.random.permutation(key, blocks)[partner]
    strong = (owner == chosen) | (owner == (partner + blocks // 2) % blocks)
    return jnp.where(strong, factor * drawn, drawn)


def block_levels(key, dims, shards, least, high):
    factor_of = 1.0
    for axis_at, parts in shards:
        draws = jax.random.uniform(jax.random.fold_in(jax.random.fold_in(key, 6), axis_at), (parts,), jnp.float32, least / len(shards), high / len(shards))
        factor_of = factor_of * jnp.repeat(jnp.exp(draws), dims[axis_at] // parts).reshape((-1,) + (1,) * (len(dims) - 1 - axis_at))
    return factor_of


def normal_values(own_key, extent, width, most, split=(), kind=jnp.bfloat16):
    drawn = width * jax.random.normal(own_key, extent, jnp.float32)
    if split:
        drawn = drawn * block_levels(own_key, extent, split, -0.22, 0.18)
    return jnp.clip(drawn, -most, most).astype(kind)


def gaussian_with(rng, dims, width, most, pieces, heavy, held_as=jnp.bfloat16):
    values = width * jax.random.normal(rng, dims, jnp.float32)
    if pieces:
        values = values * block_levels(rng, dims, pieces, -0.22, 0.18)
    return jnp.clip(spiked(values, jax.random.fold_in(rng, 3), *heavy), -most, most).astype(held_as)


def setup_inputs(seed: int = 0, part: int = 0) -> dict:
    key_of = jax.random.split(jax.random.key(seed), 6)
    own_keys = jax.random.split(jax.random.fold_in(key_of[5], part), 6)
    opacity_deriv = gaussian_with(own_keys[0], (LINES, CELLS, BANDS), 1.0, 6.0, ((2, 16),), (2, 1, 16, 2.0))
    emission_deriv = normal_values(own_keys[1], (LINES, CELLS, BANDS), BANDS ** -0.5, 0.09375, ((2, 16),))
    kernel_tiles = jnp.clip(jax.random.uniform(key_of[2], (KINDS, TILE, TILE), jnp.float32, 0.1, 1.0), 0.1, 1.0)
    tile_map = set_ends(jax.random.randint(own_keys[3], (LINES, BLOCKS, BLOCKS), 0, KINDS), jax.random.fold_in(own_keys[3], 1), 0, KINDS - 1).astype(jnp.int32)
    active_counts = draw_active_counts(jax.random.fold_in(jax.random.fold_in(key_of[5], part), 71), part)
    return {"opacity_deriv": opacity_deriv, "emission_deriv": emission_deriv, "kernel_tiles": kernel_tiles, "tile_map": tile_map, "active_counts": active_counts}


def reference(opacity_deriv, emission_deriv, kernel_tiles, tile_map, active_counts):
    coupling = jnp.einsum("lib,ljb->ilj", opacity_deriv.astype(jnp.float32), emission_deriv.astype(jnp.float32))
    tiles = kernel_tiles[tile_map]
    weight = jnp.transpose(tiles, (0, 1, 3, 2, 4)).reshape(LINES, CELLS, CELLS)
    weight = jnp.transpose(weight, (1, 0, 2))
    cell_index = jnp.arange(CELLS, dtype=jnp.int32)
    same = (cell_index[:, None, None] == cell_index[None, None, :]).astype(jnp.float32)
    diagonal = jnp.sum(coupling * same, axis=2, keepdims=True)
    live = active_counts[None, :, None]
    inside = (cell_index[:, None, None] < live) & (cell_index[None, None, :] < live)
    result = weight * coupling - 2.0 * same * diagonal
    return jnp.where(inside, result, jnp.zeros_like(result))
```

```python
import functools

import jax
import jax.numpy as jnp
from jax import lax
from jax.experimental import pallas as pl
from jax.experimental.pallas import tpu as pltpu
from jax.sharding import PartitionSpec as P

MESH = pl.DeviceIdType.MESH
TOP = 32767.0
TINY = 1e-30
WIDTH = 256


def plain_body(opacity_deriv, emission_deriv, kernel_tiles, tile_map, active_counts):
    cells = opacity_deriv.shape[1]
    kinds = kernel_tiles.shape[0]
    tile = kernel_tiles.shape[1]
    shards = lax.axis_size("band")
    row_count = cells // shards
    first_row = lax.axis_index("band") * row_count
    coupling = lax.psum_scatter(
        jnp.einsum(
            "lib,ljb->ilj", opacity_deriv, emission_deriv, preferred_element_type=jnp.float32
        ),
        "band",
        scatter_dimension=0,
        tiled=True,
    )
    my_rows = first_row + jnp.arange(row_count, dtype=jnp.int32)
    chosen = jnp.take(tile_map, my_rows // tile, axis=1)
    onehot = (chosen[..., None] == jnp.arange(kinds, dtype=jnp.int32)).astype(jnp.float32)
    tile_rows = jnp.take(kernel_tiles, my_rows % tile, axis=1)
    weight = jnp.einsum("lrqk,krt->rlqt", onehot, tile_rows, precision=lax.Precision.HIGHEST)
    weight = weight.reshape(row_count, onehot.shape[0], cells)
    columns = jnp.arange(cells, dtype=jnp.int32)
    same = (my_rows[:, None, None] == columns[None, None, :]).astype(jnp.float32)
    diagonal = jnp.sum(coupling * same, axis=2, keepdims=True)
    live = active_counts[None, :, None]
    inside = (my_rows[:, None, None] < live) & (columns[None, None, :] < live)
    result = weight * coupling - 2.0 * same * diagonal
    return jnp.where(inside, result, jnp.zeros_like(result))


def encode(block):
    top = jnp.maximum(jnp.max(jnp.abs(block), axis=0, keepdims=True), TINY)
    coded = jnp.round(block * (TOP / top)).astype(jnp.int32).astype(jnp.int16)
    return coded, top * (1.0 / TOP)


def decode(coded, scale):
    return coded.astype(jnp.int32).astype(jnp.float32) * scale


def product(left, right):
    return lax.dot_general(
        left, right, (((1,), (1,)), ((), ())), preferred_element_type=jnp.float32
    )


def kernel(
    op_ref, em_ref, kt_ref, tm_ref, ac_ref, out_ref,
    a_own, a_mate, b_own, b_mate, tiles,
    y_out, y_out_scale, y_in, y_in_scale,
    z_out, z_out_scale, z_in, z_in_scale, total,
    own_sem, mate_send, mate_recv, y_send, y_recv, z_send, z_recv,
):
    lines, cells = em_ref.shape[0], em_ref.shape[1]
    rows = op_ref.shape[3]
    tile = kt_ref.shape[2]
    depth = total.shape[0] // lines
    levels = op_ref.shape[1] // 2
    me = lax.axis_index("band")
    core = lax.rem(me, 2)
    y = lax.rem(me // 2, 2)
    z = me // 4
    mate = z * 4 + y * 2 + (1 - core)
    across = z * 4 + (1 - y) * 2 + core
    z_of = [lax.rem(z + d, levels) for d in range(levels)]
    along = [z_of[d] * 4 + y * 2 + core for d in range(levels)]

    own_copies = []
    for l in range(lines):
        own_copies.append(
            (
                pltpu.make_async_copy(op_ref.at[l, :, core], a_own.at[l], own_sem.at[l, 0]),
                pltpu.make_async_copy(em_ref.at[l], b_own.at[l], own_sem.at[l, 1]),
            )
        )
    tile_copy = pltpu.make_async_copy(
        kt_ref.at[:, pl.ds(pl.multiple_of(core * rows, rows), rows), :], tiles, own_sem.at[0, 2]
    )
    for pair in own_copies:
        for copy in pair:
            copy.start()
    tile_copy.start()

    barrier = pltpu.get_barrier_semaphore()
    peers = [mate, across] + along[1:]
    for peer in peers:
        pl.semaphore_signal(barrier, inc=1, device_id={"band": peer}, device_id_type=MESH)
    pl.semaphore_wait(barrier, len(peers))

    mate_copies = []
    for l in range(lines):
        mate_copies.append(
            (
                pltpu.make_async_remote_copy(
                    op_ref.at[l, :, 1 - core], a_mate.at[l], mate_send.at[l, 0], mate_recv.at[l, 0],
                    device_id={"band": mate}, device_id_type=MESH,
                ),
                pltpu.make_async_remote_copy(
                    em_ref.at[l], b_mate.at[l], mate_send.at[l, 1], mate_recv.at[l, 1],
                    device_id={"band": mate}, device_id_type=MESH,
                ),
            )
        )
    for pair in mate_copies:
        for copy in pair:
            copy.start()

    def partial_sum(l, column, side):
        left_own = jnp.concatenate([a_own[l, z_of[d] * 2 + side] for d in range(levels)], axis=0)
        left_mate = jnp.concatenate([a_mate[l, z_of[d] * 2 + side] for d in range(levels)], axis=0)
        span = pl.ds(column, WIDTH)
        return product(left_own, b_own[l, span, :]) + product(left_mate, b_mate[l, span, :])

    def y_copies(step):
        return (
            pltpu.make_async_remote_copy(
                y_out.at[step], y_in.at[step], y_send.at[step, 0], y_recv.at[step, 0],
                device_id={"band": across}, device_id_type=MESH,
            ),
            pltpu.make_async_remote_copy(
                y_out_scale.at[step], y_in_scale.at[step], y_send.at[step, 1], y_recv.at[step, 1],
                device_id={"band": across}, device_id_type=MESH,
            ),
        )

    def z_copies(step, d):
        return (
            pltpu.make_async_remote_copy(
                z_out.at[step, d - 1], z_in.at[step, d - 1],
                z_send.at[step, d - 1, 0], z_recv.at[step, d - 1, 0],
                device_id={"band": along[d]}, device_id_type=MESH,
            ),
            pltpu.make_async_remote_copy(
                z_out_scale.at[step, d - 1], z_in_scale.at[step, d - 1],
                z_send.at[step, d - 1, 1], z_recv.at[step, d - 1, 1],
                device_id={"band": along[d]}, device_id_type=MESH,
            ),
        )

    for l in range(lines):
        for copy in own_copies[l] + mate_copies[l]:
            copy.wait()

        @pl.loop(0, depth)
        def _(part):
            step = l * depth + part
            column = pl.multiple_of(part * WIDTH, WIDTH)
            sums = partial_sum(l, column, 1 - y)
            for d in range(levels):
                coded, scale = encode(sums[d * rows : (d + 1) * rows])
                y_out[step, d] = coded
                y_out_scale[step, d : d + 1] = scale
            for copy in y_copies(step):
                copy.start()

    for l in range(lines):

        @pl.loop(0, depth)
        def _(part):
            step = l * depth + part
            column = pl.multiple_of(part * WIDTH, WIDTH)
            sums = partial_sum(l, column, y)
            for copy in y_copies(step):
                copy.wait()
            for d in list(range(1, levels)) + [0]:
                block = sums[d * rows : (d + 1) * rows] + decode(
                    y_in[step, d], y_in_scale[step, d : d + 1]
                )
                if d == 0:
                    total[step] = block
                else:
                    coded, scale = encode(block)
                    z_out[step, d - 1] = coded
                    z_out_scale[step, d - 1] = scale
                    for copy in z_copies(step, d):
                        copy.start()

    tile_copy.wait()
    row = lax.broadcasted_iota(jnp.int32, (rows, tile), 0) + me * rows
    lane = lax.broadcasted_iota(jnp.int32, (rows, tile), 1)
    for l in range(lines):
        live = ac_ref[l]

        @pl.loop(0, depth)
        def _(part):
            step = l * depth + part
            block = total[step]
            for d in range(1, levels):
                for copy in z_copies(step, d):
                    copy.wait()
                block = block + decode(z_in[step, d - 1], z_in_scale[step, d - 1])
            for s in range(WIDTH // tile):
                coupling = block[:, s * tile : (s + 1) * tile]
                at = part * (WIDTH // tile) + s
                weight = tiles[tm_ref[l, me // 2, at]]
                column = lane + at * tile
                result = weight * coupling
                result = jnp.where(row == column, result - 2.0 * coupling, result)
                inside = (row < live) & (column < live)
                start = pl.multiple_of(l * cells + at * tile, tile)
                out_ref[:, pl.ds(start, tile)] = jnp.where(inside, result, 0.0)


def fused_body(opacity_deriv, emission_deriv, kernel_tiles, tile_map, active_counts):
    lines, cells, bands = opacity_deriv.shape
    kinds, tile, _ = kernel_tiles.shape
    shards = lax.axis_size("band")
    rows = cells // shards
    levels = shards // 4
    groups = shards // 2
    steps = lines * (cells // WIDTH)
    vmem = pltpu.VMEM
    dma = pltpu.SemaphoreType.DMA
    half = jnp.bfloat16
    wide = jnp.float32
    out = pl.pallas_call(
        kernel,
        out_shape=jax.ShapeDtypeStruct((rows, lines * cells), wide),
        in_specs=[pl.BlockSpec(memory_space=pl.ANY)] * 3
        + [pl.BlockSpec(memory_space=pltpu.SMEM)] * 2,
        out_specs=pl.BlockSpec(memory_space=pltpu.VMEM),
        scratch_shapes=[
            vmem((lines, groups, rows, bands), half),
            vmem((lines, groups, rows, bands), half),
            vmem((lines, cells, bands), half),
            vmem((lines, cells, bands), half),
            vmem((kinds, rows, tile), wide),
            vmem((steps, levels, rows, WIDTH), jnp.int16),
            vmem((steps, levels, WIDTH), wide),
            vmem((steps, levels, rows, WIDTH), jnp.int16),
            vmem((steps, levels, WIDTH), wide),
            vmem((steps, levels - 1, rows, WIDTH), jnp.int16),
            vmem((steps, levels - 1, 1, WIDTH), wide),
            vmem((steps, levels - 1, rows, WIDTH), jnp.int16),
            vmem((steps, levels - 1, 1, WIDTH), wide),
            vmem((steps, rows, WIDTH), wide),
            dma((lines, 3)),
            dma((lines, 2)),
            dma((lines, 2)),
            dma((steps, 2)),
            dma((steps, 2)),
            dma((steps, levels - 1, 2)),
            dma((steps, levels - 1, 2)),
        ],
        compiler_params=pltpu.CompilerParams(
            collective_id=0, has_side_effects=True, vmem_limit_bytes=40 * 1024 * 1024
        ),
        cost_estimate=pl.CostEstimate(
            flops=2 * lines * cells * cells * bands,
            bytes_accessed=4 * lines * cells * bands,
            transcendentals=0,
        ),
        name="band_sum",
    )(
        opacity_deriv.reshape(lines, groups, 2, rows, bands),
        emission_deriv,
        kernel_tiles,
        tile_map,
        active_counts,
    )
    return out.reshape(rows, lines, cells)


def solution(mesh):
    body = fused_body if mesh.shape["band"] == 16 else plain_body
    return jax.shard_map(
        body,
        mesh=mesh,
        in_specs=(
            P("grp", None, "band"),
            P("grp", None, "band"),
            P(),
            P("grp", None, None),
            P("grp"),
        ),
        out_specs=P("band", "grp", None),
        check_vma=False,
    )
```

```python
import functools

import jax
import jax.numpy as jnp
from jax import lax
from jax.experimental import pallas as pl
from jax.experimental.pallas import tpu as pltpu
from jax.sharding import PartitionSpec as P

MESH = pl.DeviceIdType.MESH
TOP = 32767.0
TINY = 1e-30
WIDTH = 256
LAG_ALONG = 2
LAG_FINISH = 2
FAR_FIRST = (2, 1, 3, 0)


def plain_body(opacity_deriv, emission_deriv, kernel_tiles, tile_map, active_counts):
    cells = opacity_deriv.shape[1]
    kinds = kernel_tiles.shape[0]
    tile = kernel_tiles.shape[1]
    shards = lax.axis_size("band")
    row_count = cells // shards
    first_row = lax.axis_index("band") * row_count
    coupling = lax.psum_scatter(
        jnp.einsum(
            "lib,ljb->ilj", opacity_deriv, emission_deriv, preferred_element_type=jnp.float32
        ),
        "band",
        scatter_dimension=0,
        tiled=True,
    )
    my_rows = first_row + jnp.arange(row_count, dtype=jnp.int32)
    chosen = jnp.take(tile_map, my_rows // tile, axis=1)
    onehot = (chosen[..., None] == jnp.arange(kinds, dtype=jnp.int32)).astype(jnp.float32)
    tile_rows = jnp.take(kernel_tiles, my_rows % tile, axis=1)
    weight = jnp.einsum("lrqk,krt->rlqt", onehot, tile_rows, precision=lax.Precision.HIGHEST)
    weight = weight.reshape(row_count, onehot.shape[0], cells)
    columns = jnp.arange(cells, dtype=jnp.int32)
    same = (my_rows[:, None, None] == columns[None, None, :]).astype(jnp.float32)
    diagonal = jnp.sum(coupling * same, axis=2, keepdims=True)
    live = active_counts[None, :, None]
    inside = (my_rows[:, None, None] < live) & (columns[None, None, :] < live)
    result = weight * coupling - 2.0 * same * diagonal
    return jnp.where(inside, result, jnp.zeros_like(result))


def encode(block):
    top = jnp.maximum(jnp.max(jnp.abs(block), axis=0, keepdims=True), TINY)
    coded = jnp.round(block * (TOP / top)).astype(jnp.int32).astype(jnp.int16)
    return coded, top * (1.0 / TOP)


def decode(coded, scale):
    return coded.astype(jnp.int32).astype(jnp.float32) * scale


def product(left, right):
    return lax.dot_general(
        left, right, (((1,), (1,)), ((), ())), preferred_element_type=jnp.float32
    )


def kernel(
    op_ref, em_ref, kt_ref, map_ref, counts_ref, out_ref,
    a_own, a_mate, b_own, b_mate, tiles, tm_ref, ac_ref,
    y_out, y_out_scale, y_in, y_in_scale,
    z_out, z_out_scale, z_in, z_in_scale, total,
    own_sem, table_sem, a_send, a_recv, b_send, b_recv, y_send, y_recv, z_send, z_recv,
):
    lines, cells = em_ref.shape[0], em_ref.shape[1]
    levels, rows = op_ref.shape[1], op_ref.shape[4]
    tile = kt_ref.shape[2]
    steps = total.shape[0]
    depth = steps // lines
    me = lax.axis_index("band")
    core = lax.rem(me, 2)
    y = lax.rem(me // 2, 2)
    z = me // 4
    mate = z * 4 + y * 2 + (1 - core)
    across = z * 4 + (1 - y) * 2 + core
    z_of = [lax.rem(z + d, levels) for d in range(levels)]
    along = [z_of[d] * 4 + y * 2 + core for d in range(levels)]

    def place(step):
        l = step // depth
        return l, pl.multiple_of((step - l * depth) * WIDTH, WIDTH)

    own_copies = [
        pltpu.make_async_copy(op_ref.at[l, :, side, core], a_own.at[l, side], own_sem.at[l, side])
        for l in range(lines)
        for side in range(2)
    ] + [pltpu.make_async_copy(em_ref.at[l], b_own.at[l], own_sem.at[l, 2]) for l in range(lines)]
    table_copies = [
        pltpu.make_async_copy(
            kt_ref.at[:, pl.ds(pl.multiple_of(core * rows, rows), rows), :], tiles, table_sem.at[0]
        ),
        pltpu.make_async_copy(map_ref, tm_ref, table_sem.at[1]),
        pltpu.make_async_copy(counts_ref, ac_ref, table_sem.at[2]),
    ]

    barrier = pltpu.get_barrier_semaphore()
    peers = [mate, across] + along[1:]
    for peer in peers:
        pl.semaphore_signal(barrier, inc=1, device_id={"band": peer}, device_id_type=MESH)
    for copy in own_copies + table_copies:
        copy.start()
    pl.semaphore_wait(barrier, len(peers))

    def a_copy(l, side):
        return pltpu.make_async_remote_copy(
            op_ref.at[l, :, side, 1 - core], a_mate.at[l, side],
            a_send.at[l, side], a_recv.at[l, side],
            device_id={"band": mate}, device_id_type=MESH,
        )

    def b_copy(step):
        l, column = place(step)
        span = pl.ds(column, WIDTH)
        return pltpu.make_async_remote_copy(
            em_ref.at[l, span, :], b_mate.at[l, span, :], b_send.at[step], b_recv.at[step],
            device_id={"band": mate}, device_id_type=MESH,
        )

    def y_copies(step):
        return (
            pltpu.make_async_remote_copy(
                y_out.at[step], y_in.at[step], y_send.at[step, 0], y_recv.at[step, 0],
                device_id={"band": across}, device_id_type=MESH,
            ),
            pltpu.make_async_remote_copy(
                y_out_scale.at[step], y_in_scale.at[step], y_send.at[step, 1], y_recv.at[step, 1],
                device_id={"band": across}, device_id_type=MESH,
            ),
        )

    def z_copies(step, d):
        return (
            pltpu.make_async_remote_copy(
                z_out.at[step, d - 1], z_in.at[step, d - 1],
                z_send.at[step, d - 1, 0], z_recv.at[step, d - 1, 0],
                device_id={"band": along[d]}, device_id_type=MESH,
            ),
            pltpu.make_async_remote_copy(
                z_out_scale.at[step, d - 1], z_in_scale.at[step, d - 1],
                z_send.at[step, d - 1, 1], z_recv.at[step, d - 1, 1],
                device_id={"band": along[d]}, device_id_type=MESH,
            ),
        )

    for l in range(lines):
        a_copy(l, 1 - y).start()
        b_copy(l * depth).start()
        if l == 0:
            a_copy(l, y).start()

        @pl.loop(1, depth)
        def _(part):
            b_copy(l * depth + part).start()

        if l > 0:
            a_copy(l, y).start()

    for copy in own_copies + table_copies:
        copy.wait()

    def partial_sum(step, side):
        l, column = place(step)
        left_own = jnp.concatenate([a_own[l, side, z_of[d]] for d in range(levels)], axis=0)
        left_mate = jnp.concatenate([a_mate[l, side, z_of[d]] for d in range(levels)], axis=0)
        span = pl.ds(column, WIDTH)
        return product(left_own, b_own[l, span, :]) + product(left_mate, b_mate[l, span, :])

    def send_across(step):
        l, column = place(step)

        @pl.when(column == 0)
        def _():
            a_copy(l, 1 - y).wait()

        b_copy(step).wait()
        sums = partial_sum(step, 1 - y)
        for d in range(levels):
            coded, scale = encode(sums[d * rows : (d + 1) * rows])
            y_out[step, d] = coded
            y_out_scale[step, d : d + 1] = scale
        for copy in y_copies(step):
            copy.start()

    def send_along(step):
        l, column = place(step)

        @pl.when(column == 0)
        def _():
            a_copy(l, y).wait()

        sums = partial_sum(step, y)
        for copy in y_copies(step):
            copy.wait()
        for d in FAR_FIRST:
            block = sums[d * rows : (d + 1) * rows] + decode(
                y_in[step, d], y_in_scale[step, d : d + 1]
            )
            if d == 0:
                total[step] = block
            else:
                coded, scale = encode(block)
                z_out[step, d - 1] = coded
                z_out_scale[step, d - 1] = scale
                for copy in z_copies(step, d):
                    copy.start()

    row = lax.broadcasted_iota(jnp.int32, (rows, tile), 0) + me * rows
    lane = lax.broadcasted_iota(jnp.int32, (rows, tile), 1)

    def finish(step):
        l, first = place(step)
        live = ac_ref[l]
        block = total[step]
        for d in range(1, levels):
            for copy in z_copies(step, d):
                copy.wait()
            block = block + decode(z_in[step, d - 1], z_in_scale[step, d - 1])
        for s in range(WIDTH // tile):
            coupling = block[:, s * tile : (s + 1) * tile]
            weight = tiles[tm_ref[l, me // 2, first // tile + s]]
            column = lane + (first + s * tile)
            result = weight * coupling
            result = jnp.where(row == column, result - 2.0 * coupling, result)
            inside = (row < live) & (column < live)
            start = pl.multiple_of(l * cells + first + s * tile, tile)
            out_ref[:, pl.ds(start, tile)] = jnp.where(inside, result, 0.0)

    @pl.loop(0, steps + LAG_ALONG + LAG_FINISH)
    def _(turn):
        @pl.when(turn < steps)
        def _():
            send_across(turn)

        @pl.when((turn >= LAG_ALONG) & (turn < steps + LAG_ALONG))
        def _():
            send_along(turn - LAG_ALONG)

        @pl.when(turn >= LAG_ALONG + LAG_FINISH)
        def _():
            finish(turn - (LAG_ALONG + LAG_FINISH))


def fused_body(opacity_deriv, emission_deriv, kernel_tiles, tile_map, active_counts):
    lines, cells, bands = opacity_deriv.shape
    kinds, tile, _ = kernel_tiles.shape
    shards = lax.axis_size("band")
    rows = cells // shards
    levels = shards // 4
    steps = lines * (cells // WIDTH)
    vmem = pltpu.VMEM
    dma = pltpu.SemaphoreType.DMA
    half = jnp.bfloat16
    wide = jnp.float32
    out = pl.pallas_call(
        kernel,
        out_shape=jax.ShapeDtypeStruct((rows, lines * cells), wide),
        in_specs=[pl.BlockSpec(memory_space=pltpu.HBM)] * 5,
        out_specs=pl.BlockSpec(memory_space=pltpu.VMEM),
        scratch_shapes=[
            vmem((lines, 2, levels, rows, bands), half),
            vmem((lines, 2, levels, rows, bands), half),
            vmem((lines, cells, bands), half),
            vmem((lines, cells, bands), half),
            vmem((kinds, rows, tile), wide),
            pltpu.SMEM(tile_map.shape, tile_map.dtype),
            pltpu.SMEM(active_counts.shape, active_counts.dtype),
            vmem((steps, levels, rows, WIDTH), jnp.int16),
            vmem((steps, levels, WIDTH), wide),
            vmem((steps, levels, rows, WIDTH), jnp.int16),
            vmem((steps, levels, WIDTH), wide),
            vmem((steps, levels - 1, rows, WIDTH), jnp.int16),
            vmem((steps, levels - 1, 1, WIDTH), wide),
            vmem((steps, levels - 1, rows, WIDTH), jnp.int16),
            vmem((steps, levels - 1, 1, WIDTH), wide),
            vmem((steps, rows, WIDTH), wide),
            dma((lines, 3)),
            dma((3,)),
            dma((lines, 2)),
            dma((lines, 2)),
            dma((steps,)),
            dma((steps,)),
            dma((steps, 2)),
            dma((steps, 2)),
            dma((steps, levels - 1, 2)),
            dma((steps, levels - 1, 2)),
        ],
        compiler_params=pltpu.CompilerParams(
            collective_id=0, has_side_effects=True, vmem_limit_bytes=62 * 1024 * 1024
        ),
        cost_estimate=pl.CostEstimate(
            flops=2 * lines * cells * cells * bands,
            bytes_accessed=4 * lines * cells * bands,
            transcendentals=0,
        ),
        name="band_sum",
    )(
        opacity_deriv.reshape(lines, levels, 2, 2, rows, bands),
        emission_deriv,
        kernel_tiles,
        tile_map,
        active_counts,
    )
    return out.reshape(rows, lines, cells)


def solution(mesh):
    body = fused_body if mesh.shape["band"] == 16 else plain_body
    return jax.shard_map(
        body,
        mesh=mesh,
        in_specs=(
            P("grp", None, "band"),
            P("grp", None, "band"),
            P(),
            P("grp", None, None),
            P("grp"),
        ),
        out_specs=P("band", "grp", None),
        check_vma=False,
    )
```

```python
import functools

import jax
import jax.numpy as jnp
from jax import lax
from jax.experimental import pallas as pl
from jax.experimental.pallas import tpu as pltpu
from jax.sharding import PartitionSpec as P

MESH = pl.DeviceIdType.MESH
TOP = 32767.0
TINY = 1e-30
WIDTH = 256
LAG_ALONG = 2
LAG_FINISH = 2
FAR_FIRST = (2, 1, 3, 0)


def plain_body(opacity_deriv, emission_deriv, kernel_tiles, tile_map, active_counts):
    cells = opacity_deriv.shape[1]
    kinds = kernel_tiles.shape[0]
    tile = kernel_tiles.shape[1]
    shards = lax.axis_size("band")
    row_count = cells // shards
    first_row = lax.axis_index("band") * row_count
    coupling = lax.psum_scatter(
        jnp.einsum(
            "lib,ljb->ilj", opacity_deriv, emission_deriv, preferred_element_type=jnp.float32
        ),
        "band",
        scatter_dimension=0,
        tiled=True,
    )
    my_rows = first_row + jnp.arange(row_count, dtype=jnp.int32)
    chosen = jnp.take(tile_map, my_rows // tile, axis=1)
    onehot = (chosen[..., None] == jnp.arange(kinds, dtype=jnp.int32)).astype(jnp.float32)
    tile_rows = jnp.take(kernel_tiles, my_rows % tile, axis=1)
    weight = jnp.einsum("lrqk,krt->rlqt", onehot, tile_rows, precision=lax.Precision.HIGHEST)
    weight = weight.reshape(row_count, onehot.shape[0], cells)
    columns = jnp.arange(cells, dtype=jnp.int32)
    same = (my_rows[:, None, None] == columns[None, None, :]).astype(jnp.float32)
    diagonal = jnp.sum(coupling * same, axis=2, keepdims=True)
    live = active_counts[None, :, None]
    inside = (my_rows[:, None, None] < live) & (columns[None, None, :] < live)
    result = weight * coupling - 2.0 * same * diagonal
    return jnp.where(inside, result, jnp.zeros_like(result))


def encode(block):
    top = jnp.maximum(jnp.max(jnp.abs(block), axis=0, keepdims=True), TINY)
    coded = jnp.round(block * (TOP / top)).astype(jnp.int32).astype(jnp.int16)
    return coded, top * (1.0 / TOP)


def decode(coded, scale):
    return coded.astype(jnp.int32).astype(jnp.float32) * scale


def product(left, right):
    return lax.dot_general(
        left, right, (((1,), (1,)), ((), ())), preferred_element_type=jnp.float32
    )


def kernel(
    op_ref, em_ref, kt_ref, map_ref, counts_ref, out_ref,
    a_own, a_mate, b_own, b_mate, tiles, tm_ref, ac_ref,
    y_out, y_out_scale, y_in, y_in_scale,
    z_out, z_out_scale, z_in, z_in_scale, total,
    own_sem, table_sem, a_send, a_recv, b_send, b_recv, y_send, y_recv, z_send, z_recv,
):
    lines, cells = em_ref.shape[0], em_ref.shape[1]
    levels, rows = op_ref.shape[1], op_ref.shape[4]
    tile = kt_ref.shape[2]
    steps = total.shape[0]
    depth = steps // lines
    me = lax.axis_index("band")
    core = lax.rem(me, 2)
    y = lax.rem(me // 2, 2)
    z = me // 4
    mate = z * 4 + y * 2 + (1 - core)
    across = z * 4 + (1 - y) * 2 + core
    z_of = [lax.rem(z + d, levels) for d in range(levels)]
    along = [z_of[d] * 4 + y * 2 + core for d in range(levels)]

    def place(step):
        l = step // depth
        return l, pl.multiple_of((step - l * depth) * WIDTH, WIDTH)

    own_copies = [
        pltpu.make_async_copy(op_ref.at[l, :, side, core], a_own.at[l, side], own_sem.at[l, side])
        for l in range(lines)
        for side in range(2)
    ] + [pltpu.make_async_copy(em_ref.at[l], b_own.at[l], own_sem.at[l, 2]) for l in range(lines)]
    table_copies = [
        pltpu.make_async_copy(
            kt_ref.at[:, pl.ds(pl.multiple_of(core * rows, rows), rows), :], tiles, table_sem.at[0]
        ),
        pltpu.make_async_copy(map_ref, tm_ref, table_sem.at[1]),
        pltpu.make_async_copy(counts_ref, ac_ref, table_sem.at[2]),
    ]

    barrier = pltpu.get_barrier_semaphore()
    peers = [mate, across] + along[1:]
    for peer in peers:
        pl.semaphore_signal(barrier, inc=1, device_id={"band": peer}, device_id_type=MESH)
    for copy in own_copies + table_copies:
        copy.start()
    pl.semaphore_wait(barrier, len(peers))

    def a_copy(l, side):
        return pltpu.make_async_remote_copy(
            op_ref.at[l, :, side, 1 - core], a_mate.at[l, side],
            a_send.at[l, side], a_recv.at[l, side],
            device_id={"band": mate}, device_id_type=MESH,
        )

    def b_copy(step):
        l, column = place(step)
        span = pl.ds(column, WIDTH)
        return pltpu.make_async_remote_copy(
            em_ref.at[l, span, :], b_mate.at[l, span, :], b_send.at[step], b_recv.at[step],
            device_id={"band": mate}, device_id_type=MESH,
        )

    def y_copies(step):
        return (
            pltpu.make_async_remote_copy(
                y_out.at[step], y_in.at[step], y_send.at[step, 0], y_recv.at[step, 0],
                device_id={"band": across}, device_id_type=MESH,
            ),
            pltpu.make_async_remote_copy(
                y_out_scale.at[step], y_in_scale.at[step], y_send.at[step, 1], y_recv.at[step, 1],
                device_id={"band": across}, device_id_type=MESH,
            ),
        )

    def z_copies(step, d):
        return (
            pltpu.make_async_remote_copy(
                z_out.at[step, d - 1], z_in.at[step, d - 1],
                z_send.at[step, d - 1, 0], z_recv.at[step, d - 1, 0],
                device_id={"band": along[d]}, device_id_type=MESH,
            ),
            pltpu.make_async_remote_copy(
                z_out_scale.at[step, d - 1], z_in_scale.at[step, d - 1],
                z_send.at[step, d - 1, 1], z_recv.at[step, d - 1, 1],
                device_id={"band": along[d]}, device_id_type=MESH,
            ),
        )

    for l in range(lines):
        a_copy(l, 1 - y).start()
        b_copy(l * depth).start()
        if l == 0:
            a_copy(l, y).start()

        @pl.loop(1, depth)
        def _(part):
            b_copy(l * depth + part).start()

        if l > 0:
            a_copy(l, y).start()

    for copy in own_copies + table_copies:
        copy.wait()

    def partial_sum(step, side):
        l, column = place(step)
        left_own = jnp.concatenate([a_own[l, side, z_of[d]] for d in range(levels)], axis=0)
        left_mate = jnp.concatenate([a_mate[l, side, z_of[d]] for d in range(levels)], axis=0)
        span = pl.ds(column, WIDTH)
        return product(left_own, b_own[l, span, :]) + product(left_mate, b_mate[l, span, :])

    def send_across(step):
        l, column = place(step)

        @pl.when(column == 0)
        def _():
            a_copy(l, 1 - y).wait()

        b_copy(step).wait()
        sums = partial_sum(step, 1 - y)
        for d in range(levels):
            coded, scale = encode(sums[d * rows : (d + 1) * rows])
            y_out[step, d] = coded
            y_out_scale[step, d : d + 1] = scale
        for copy in y_copies(step):
            copy.start()

    def send_along(step):
        l, column = place(step)

        @pl.when(column == 0)
        def _():
            a_copy(l, y).wait()

        sums = partial_sum(step, y)
        for copy in y_copies(step):
            copy.wait()
        for d in FAR_FIRST:
            block = sums[d * rows : (d + 1) * rows] + decode(
                y_in[step, d], y_in_scale[step, d : d + 1]
            )
            if d == 0:
                total[step] = block
            else:
                coded, scale = encode(block)
                z_out[step, d - 1] = coded
                z_out_scale[step, d - 1] = scale
                for copy in z_copies(step, d):
                    copy.start()

    row = lax.broadcasted_iota(jnp.int32, (rows, tile), 0) + me * rows
    lane = lax.broadcasted_iota(jnp.int32, (rows, tile), 1)

    def finish(step):
        l, first = place(step)
        live = ac_ref[l]
        block = total[step]
        for d in range(1, levels):
            for copy in z_copies(step, d):
                copy.wait()
            block = block + decode(z_in[step, d - 1], z_in_scale[step, d - 1])
        for s in range(WIDTH // tile):
            coupling = block[:, s * tile : (s + 1) * tile]
            weight = tiles[tm_ref[l, me // 2, first // tile + s]]
            column = lane + (first + s * tile)
            result = weight * coupling
            result = jnp.where(row == column, result - 2.0 * coupling, result)
            inside = (row < live) & (column < live)
            start = pl.multiple_of(l * cells + first + s * tile, tile)
            out_ref[:, pl.ds(start, tile)] = jnp.where(inside, result, 0.0)

    @pl.loop(0, steps + LAG_ALONG + LAG_FINISH)
    def _(turn):
        @pl.when(turn < steps)
        def _():
            send_across(turn)

        @pl.when((turn >= LAG_ALONG) & (turn < steps + LAG_ALONG))
        def _():
            send_along(turn - LAG_ALONG)

        @pl.when(turn >= LAG_ALONG + LAG_FINISH)
        def _():
            finish(turn - (LAG_ALONG + LAG_FINISH))


def fused_body(opacity_deriv, emission_deriv, kernel_tiles, tile_map, active_counts):
    lines, cells, bands = opacity_deriv.shape
    kinds, tile, _ = kernel_tiles.shape
    shards = lax.axis_size("band")
    rows = cells // shards
    levels = shards // 4
    steps = lines * (cells // WIDTH)
    vmem = pltpu.VMEM
    dma = pltpu.SemaphoreType.DMA
    half = jnp.bfloat16
    wide = jnp.float32
    out = pl.pallas_call(
        kernel,
        out_shape=pltpu.VMEM((rows, lines * cells), wide),
        in_specs=[pl.BlockSpec(memory_space=pltpu.HBM)] * 5,
        out_specs=pl.BlockSpec(memory_space=pltpu.VMEM),
        scratch_shapes=[
            vmem((lines, 2, levels, rows, bands), half),
            vmem((lines, 2, levels, rows, bands), half),
            vmem((lines, cells, bands), half),
            vmem((lines, cells, bands), half),
            vmem((kinds, rows, tile), wide),
            pltpu.SMEM(tile_map.shape, tile_map.dtype),
            pltpu.SMEM(active_counts.shape, active_counts.dtype),
            vmem((steps, levels, rows, WIDTH), jnp.int16),
            vmem((steps, levels, WIDTH), wide),
            vmem((steps, levels, rows, WIDTH), jnp.int16),
            vmem((steps, levels, WIDTH), wide),
            vmem((steps, levels - 1, rows, WIDTH), jnp.int16),
            vmem((steps, levels - 1, 1, WIDTH), wide),
            vmem((steps, levels - 1, rows, WIDTH), jnp.int16),
            vmem((steps, levels - 1, 1, WIDTH), wide),
            vmem((steps, rows, WIDTH), wide),
            dma((lines, 3)),
            dma((3,)),
            dma((lines, 2)),
            dma((lines, 2)),
            dma((steps,)),
            dma((steps,)),
            dma((steps, 2)),
            dma((steps, 2)),
            dma((steps, levels - 1, 2)),
            dma((steps, levels - 1, 2)),
        ],
        compiler_params=pltpu.CompilerParams(
            collective_id=0, has_side_effects=True, vmem_limit_bytes=62 * 1024 * 1024
        ),
        cost_estimate=pl.CostEstimate(
            flops=2 * lines * cells * cells * bands,
            bytes_accessed=4 * lines * cells * bands,
            transcendentals=0,
        ),
        name="band_sum",
    )(
        opacity_deriv.reshape(lines, levels, 2, 2, rows, bands),
        emission_deriv,
        kernel_tiles,
        tile_map,
        active_counts,
    )
    return out.reshape(rows, lines, cells)


def solution(mesh):
    body = fused_body if mesh.shape["band"] == 16 else plain_body
    return jax.shard_map(
        body,
        mesh=mesh,
        in_specs=(
            P("grp", None, "band"),
            P("grp", None, "band"),
            P(),
            P("grp", None, None),
            P("grp"),
        ),
        out_specs=P("band", "grp", None),
        check_vma=False,
    )
```

```python
import functools

import jax
import jax.numpy as jnp
from jax import lax
from jax.experimental import pallas as pl
from jax.experimental.pallas import tpu as pltpu
from jax.sharding import PartitionSpec as P

MESH = pl.DeviceIdType.MESH
TOP = 32767.0
TINY = 1e-30
WIDTH = 256
LAG_ALONG = 2
LAG_FINISH = 2
FIRST_ACROSS = 5
FAR_FIRST = (2, 1, 3, 0)


def plain_body(opacity_deriv, emission_deriv, kernel_tiles, tile_map, active_counts):
    cells = opacity_deriv.shape[1]
    kinds = kernel_tiles.shape[0]
    tile = kernel_tiles.shape[1]
    shards = lax.axis_size("band")
    row_count = cells // shards
    first_row = lax.axis_index("band") * row_count
    coupling = lax.psum_scatter(
        jnp.einsum(
            "lib,ljb->ilj", opacity_deriv, emission_deriv, preferred_element_type=jnp.float32
        ),
        "band",
        scatter_dimension=0,
        tiled=True,
    )
    my_rows = first_row + jnp.arange(row_count, dtype=jnp.int32)
    chosen = jnp.take(tile_map, my_rows // tile, axis=1)
    onehot = (chosen[..., None] == jnp.arange(kinds, dtype=jnp.int32)).astype(jnp.float32)
    tile_rows = jnp.take(kernel_tiles, my_rows % tile, axis=1)
    weight = jnp.einsum("lrqk,krt->rlqt", onehot, tile_rows, precision=lax.Precision.HIGHEST)
    weight = weight.reshape(row_count, onehot.shape[0], cells)
    columns = jnp.arange(cells, dtype=jnp.int32)
    same = (my_rows[:, None, None] == columns[None, None, :]).astype(jnp.float32)
    diagonal = jnp.sum(coupling * same, axis=2, keepdims=True)
    live = active_counts[None, :, None]
    inside = (my_rows[:, None, None] < live) & (columns[None, None, :] < live)
    result = weight * coupling - 2.0 * same * diagonal
    return jnp.where(inside, result, jnp.zeros_like(result))


def encode(block):
    top = jnp.maximum(jnp.max(jnp.abs(block), axis=0, keepdims=True), TINY)
    coded = jnp.round(block * (TOP / top)).astype(jnp.int32).astype(jnp.int16)
    return coded, top * (1.0 / TOP)


def decode(coded, scale):
    return coded.astype(jnp.int32).astype(jnp.float32) * scale


def product(left, right):
    return lax.dot_general(
        left, right, (((1,), (1,)), ((), ())), preferred_element_type=jnp.float32
    )


def kernel(
    op_ref, em_ref, kt_ref, map_ref, counts_ref, out_ref,
    a_own, a_mate, b_own, b_mate, tiles, tm_ref, ac_ref,
    y_out, y_out_scale, y_in, y_in_scale,
    z_out, z_out_scale, z_in, z_in_scale, total,
    f_out, f_out_scale, f_in, f_in_scale, f_own, c_out, c_out_scale, c_in, c_in_scale,
    own_sem, table_sem, a_send, a_recv, b_send, b_recv, y_send, y_recv, z_send, z_recv,
    f_send, f_recv, c_send, c_recv,
):
    lines, cells = em_ref.shape[0], em_ref.shape[1]
    levels, rows = op_ref.shape[1], op_ref.shape[4]
    tile = kt_ref.shape[2]
    steps = total.shape[0]
    depth = steps // lines
    me = lax.axis_index("band")
    core = lax.rem(me, 2)
    y = lax.rem(me // 2, 2)
    z = me // 4
    mate = z * 4 + y * 2 + (1 - core)
    across = z * 4 + (1 - y) * 2 + core
    z_of = [lax.rem(z + d, levels) for d in range(levels)]
    along = [z_of[d] * 4 + y * 2 + core for d in range(levels)]

    def place(step):
        l = step // depth
        return l, pl.multiple_of((step - l * depth) * WIDTH, WIDTH)

    own_copies = [
        pltpu.make_async_copy(op_ref.at[l, :, side, core], a_own.at[l, side], own_sem.at[l, side])
        for l in range(lines)
        for side in range(2)
    ] + [pltpu.make_async_copy(em_ref.at[l], b_own.at[l], own_sem.at[l, 2]) for l in range(lines)]
    table_copies = [
        pltpu.make_async_copy(
            kt_ref.at[:, pl.ds(pl.multiple_of(core * rows, rows), rows), :], tiles, table_sem.at[0]
        ),
        pltpu.make_async_copy(map_ref, tm_ref, table_sem.at[1]),
        pltpu.make_async_copy(counts_ref, ac_ref, table_sem.at[2]),
    ]

    barrier = pltpu.get_barrier_semaphore()
    peers = [mate, across] + along[1:]
    for peer in peers:
        pl.semaphore_signal(barrier, inc=1, device_id={"band": peer}, device_id_type=MESH)
    for copy in own_copies + table_copies:
        copy.start()
    pl.semaphore_wait(barrier, len(peers))

    def a_copy(l, side):
        return pltpu.make_async_remote_copy(
            op_ref.at[l, :, side, 1 - core], a_mate.at[l, side],
            a_send.at[l, side], a_recv.at[l, side],
            device_id={"band": mate}, device_id_type=MESH,
        )

    def b_copy(step):
        l, column = place(step)
        span = pl.ds(column, WIDTH)
        return pltpu.make_async_remote_copy(
            em_ref.at[l, span, :], b_mate.at[l, span, :], b_send.at[step], b_recv.at[step],
            device_id={"band": mate}, device_id_type=MESH,
        )

    def y_copies(step):
        return (
            pltpu.make_async_remote_copy(
                y_out.at[step], y_in.at[step], y_send.at[step, 0], y_recv.at[step, 0],
                device_id={"band": across}, device_id_type=MESH,
            ),
            pltpu.make_async_remote_copy(
                y_out_scale.at[step], y_in_scale.at[step], y_send.at[step, 1], y_recv.at[step, 1],
                device_id={"band": across}, device_id_type=MESH,
            ),
        )

    def z_copies(step, d):
        return (
            pltpu.make_async_remote_copy(
                z_out.at[step, d - 1], z_in.at[step, d - 1],
                z_send.at[step, d - 1, 0], z_recv.at[step, d - 1, 0],
                device_id={"band": along[d]}, device_id_type=MESH,
            ),
            pltpu.make_async_remote_copy(
                z_out_scale.at[step, d - 1], z_in_scale.at[step, d - 1],
                z_send.at[step, d - 1, 1], z_recv.at[step, d - 1, 1],
                device_id={"band": along[d]}, device_id_type=MESH,
            ),
        )

    def f_copies(d):
        return (
            pltpu.make_async_remote_copy(
                f_out.at[d - 1], f_in.at[d - 1], f_send.at[d - 1, 0], f_recv.at[d - 1, 0],
                device_id={"band": along[d]}, device_id_type=MESH,
            ),
            pltpu.make_async_remote_copy(
                f_out_scale.at[d - 1], f_in_scale.at[d - 1],
                f_send.at[d - 1, 1], f_recv.at[d - 1, 1],
                device_id={"band": along[d]}, device_id_type=MESH,
            ),
        )

    c_copies = (
        pltpu.make_async_remote_copy(
            c_out, c_in, c_send.at[0], c_recv.at[0],
            device_id={"band": across}, device_id_type=MESH,
        ),
        pltpu.make_async_remote_copy(
            c_out_scale, c_in_scale, c_send.at[1], c_recv.at[1],
            device_id={"band": across}, device_id_type=MESH,
        ),
    )

    for l in range(lines):
        a_copy(l, 1 - y).start()
        b_copy(l * depth).start()
        if l == 0:
            b_copy(1).start()
            a_copy(l, y).start()

        @pl.loop(2 if l == 0 else 1, depth)
        def _(part):
            b_copy(l * depth + part).start()

        if l > 0:
            a_copy(l, y).start()

    for copy in own_copies + table_copies:
        copy.wait()

    def partial_sum(step, side):
        l, column = place(step)
        left_own = jnp.concatenate([a_own[l, side, z_of[d]] for d in range(levels)], axis=0)
        left_mate = jnp.concatenate([a_mate[l, side, z_of[d]] for d in range(levels)], axis=0)
        span = pl.ds(column, WIDTH)
        return product(left_own, b_own[l, span, :]) + product(left_mate, b_mate[l, span, :])

    def send_across(step):
        l, column = place(step)

        @pl.when((column == 0) & (l > 0))
        def _():
            a_copy(l, 1 - y).wait()

        b_copy(step).wait()
        sums = partial_sum(step, 1 - y)
        for d in range(levels):
            coded, scale = encode(sums[d * rows : (d + 1) * rows])
            y_out[step, d] = coded
            y_out_scale[step, d : d + 1] = scale
        for copy in y_copies(step):
            copy.start()

    def send_along(step):
        l, column = place(step)

        @pl.when((column == 0) & (l > 0))
        def _():
            a_copy(l, y).wait()

        sums = partial_sum(step, y)
        for copy in y_copies(step):
            copy.wait()
        for d in FAR_FIRST:
            block = sums[d * rows : (d + 1) * rows] + decode(
                y_in[step, d], y_in_scale[step, d : d + 1]
            )
            if d == 0:
                total[step] = block
            else:
                coded, scale = encode(block)
                z_out[step, d - 1] = coded
                z_out_scale[step, d - 1] = scale
                for copy in z_copies(step, d):
                    copy.start()

    row = lax.broadcasted_iota(jnp.int32, (rows, tile), 0) + me * rows
    lane = lax.broadcasted_iota(jnp.int32, (rows, tile), 1)

    def emit(step, block):
        l, first = place(step)
        live = ac_ref[l]
        for s in range(WIDTH // tile):
            coupling = block[:, s * tile : (s + 1) * tile]
            weight = tiles[tm_ref[l, me // 2, first // tile + s]]
            column = lane + (first + s * tile)
            result = weight * coupling
            result = jnp.where(row == column, result - 2.0 * coupling, result)
            inside = (row < live) & (column < live)
            start = pl.multiple_of(l * cells + first + s * tile, tile)
            out_ref[:, pl.ds(start, tile)] = jnp.where(inside, result, 0.0)

    def finish(step):
        block = total[step]
        for d in range(1, levels):
            for copy in z_copies(step, d):
                copy.wait()
            block = block + decode(z_in[step, d - 1], z_in_scale[step, d - 1])
        emit(step, block)

    def first_along():
        a_copy(0, y).wait()
        b_copy(0).wait()
        for side in range(2):
            sums = partial_sum(0, side)
            f_own[side] = sums[:rows]
            for d in range(1, levels):
                coded, scale = encode(sums[d * rows : (d + 1) * rows])
                f_out[d - 1, side] = coded
                f_out_scale[d - 1, side] = scale
        for d in FAR_FIRST[:-1]:
            for copy in f_copies(d):
                copy.start()

    def first_sum(side):
        block = f_own[side]
        for d in range(1, levels):
            block = block + decode(f_in[d - 1, side], f_in_scale[d - 1, side])
        return block

    def first_across():
        for d in range(1, levels):
            for copy in f_copies(d):
                copy.wait()
        coded, scale = encode(first_sum(1 - y))
        c_out[...] = coded
        c_out_scale[...] = scale
        for copy in c_copies:
            copy.start()

    a_copy(0, 1 - y).wait()
    send_across(1)
    first_along()
    send_across(2)

    @pl.loop(3, steps + LAG_ALONG + LAG_FINISH)
    def _(turn):
        @pl.when(turn < steps)
        def _():
            send_across(turn)

        @pl.when((turn > LAG_ALONG) & (turn < steps + LAG_ALONG))
        def _():
            send_along(turn - LAG_ALONG)

        @pl.when(turn == FIRST_ACROSS)
        def _():
            first_across()

        @pl.when(turn > LAG_ALONG + LAG_FINISH)
        def _():
            finish(turn - (LAG_ALONG + LAG_FINISH))

        @pl.when(turn == steps)
        def _():
            for copy in c_copies:
                copy.wait()
            emit(0, first_sum(y) + decode(c_in[...], c_in_scale[...]))


def fused_body(opacity_deriv, emission_deriv, kernel_tiles, tile_map, active_counts):
    lines, cells, bands = opacity_deriv.shape
    kinds, tile, _ = kernel_tiles.shape
    shards = lax.axis_size("band")
    rows = cells // shards
    levels = shards // 4
    steps = lines * (cells // WIDTH)
    vmem = pltpu.VMEM
    dma = pltpu.SemaphoreType.DMA
    half = jnp.bfloat16
    wide = jnp.float32
    out = pl.pallas_call(
        kernel,
        out_shape=pltpu.VMEM((rows, lines * cells), wide),
        in_specs=[pl.BlockSpec(memory_space=pltpu.HBM)] * 5,
        out_specs=pl.BlockSpec(memory_space=pltpu.VMEM),
        scratch_shapes=[
            vmem((lines, 2, levels, rows, bands), half),
            vmem((lines, 2, levels, rows, bands), half),
            vmem((lines, cells, bands), half),
            vmem((lines, cells, bands), half),
            vmem((kinds, rows, tile), wide),
            pltpu.SMEM(tile_map.shape, tile_map.dtype),
            pltpu.SMEM(active_counts.shape, active_counts.dtype),
            vmem((steps, levels, rows, WIDTH), jnp.int16),
            vmem((steps, levels, WIDTH), wide),
            vmem((steps, levels, rows, WIDTH), jnp.int16),
            vmem((steps, levels, WIDTH), wide),
            vmem((steps, levels - 1, rows, WIDTH), jnp.int16),
            vmem((steps, levels - 1, 1, WIDTH), wide),
            vmem((steps, levels - 1, rows, WIDTH), jnp.int16),
            vmem((steps, levels - 1, 1, WIDTH), wide),
            vmem((steps, rows, WIDTH), wide),
            vmem((levels - 1, 2, rows, WIDTH), jnp.int16),
            vmem((levels - 1, 2, 1, WIDTH), wide),
            vmem((levels - 1, 2, rows, WIDTH), jnp.int16),
            vmem((levels - 1, 2, 1, WIDTH), wide),
            vmem((2, rows, WIDTH), wide),
            vmem((rows, WIDTH), jnp.int16),
            vmem((1, WIDTH), wide),
            vmem((rows, WIDTH), jnp.int16),
            vmem((1, WIDTH), wide),
            dma((lines, 3)),
            dma((3,)),
            dma((lines, 2)),
            dma((lines, 2)),
            dma((steps,)),
            dma((steps,)),
            dma((steps, 2)),
            dma((steps, 2)),
            dma((steps, levels - 1, 2)),
            dma((steps, levels - 1, 2)),
            dma((levels - 1, 2)),
            dma((levels - 1, 2)),
            dma((2,)),
            dma((2,)),
        ],
        compiler_params=pltpu.CompilerParams(
            collective_id=0, has_side_effects=True, vmem_limit_bytes=62 * 1024 * 1024
        ),
        cost_estimate=pl.CostEstimate(
            flops=2 * lines * cells * cells * bands,
            bytes_accessed=4 * lines * cells * bands,
            transcendentals=0,
        ),
        name="band_sum",
    )(
        opacity_deriv.reshape(lines, levels, 2, 2, rows, bands),
        emission_deriv,
        kernel_tiles,
        tile_map,
        active_counts,
    )
    return out.reshape(rows, lines, cells)


def solution(mesh):
    body = fused_body if mesh.shape["band"] == 16 else plain_body
    return jax.shard_map(
        body,
        mesh=mesh,
        in_specs=(
            P("grp", None, "band"),
            P("grp", None, "band"),
            P(),
            P("grp", None, None),
            P("grp"),
        ),
        out_specs=P("band", "grp", None),
        check_vma=False,
    )
```

```python
import functools

import jax
import jax.numpy as jnp
from jax import lax
from jax.experimental import pallas as pl
from jax.experimental.pallas import tpu as pltpu
from jax.sharding import PartitionSpec as P

MESH = pl.DeviceIdType.MESH
TOP = 32767.0
TINY = 1e-30
WIDTH = 256
LAG_ALONG = 2
LAG_FINISH = 2
FIRST_ACROSS = 5
FAR_FIRST = (2, 1, 3, 0)


def plain_body(opacity_deriv, emission_deriv, kernel_tiles, tile_map, active_counts):
    cells = opacity_deriv.shape[1]
    kinds = kernel_tiles.shape[0]
    tile = kernel_tiles.shape[1]
    shards = lax.axis_size("band")
    row_count = cells // shards
    first_row = lax.axis_index("band") * row_count
    coupling = lax.psum_scatter(
        jnp.einsum(
            "lib,ljb->ilj", opacity_deriv, emission_deriv, preferred_element_type=jnp.float32
        ),
        "band",
        scatter_dimension=0,
        tiled=True,
    )
    my_rows = first_row + jnp.arange(row_count, dtype=jnp.int32)
    chosen = jnp.take(tile_map, my_rows // tile, axis=1)
    onehot = (chosen[..., None] == jnp.arange(kinds, dtype=jnp.int32)).astype(jnp.float32)
    tile_rows = jnp.take(kernel_tiles, my_rows % tile, axis=1)
    weight = jnp.einsum("lrqk,krt->rlqt", onehot, tile_rows, precision=lax.Precision.HIGHEST)
    weight = weight.reshape(row_count, onehot.shape[0], cells)
    columns = jnp.arange(cells, dtype=jnp.int32)
    same = (my_rows[:, None, None] == columns[None, None, :]).astype(jnp.float32)
    diagonal = jnp.sum(coupling * same, axis=2, keepdims=True)
    live = active_counts[None, :, None]
    inside = (my_rows[:, None, None] < live) & (columns[None, None, :] < live)
    result = weight * coupling - 2.0 * same * diagonal
    return jnp.where(inside, result, jnp.zeros_like(result))


def encode(block):
    top = jnp.maximum(jnp.max(jnp.abs(block), axis=0, keepdims=True), TINY)
    coded = jnp.round(block * (TOP / top)).astype(jnp.int32).astype(jnp.int16)
    return coded, top * (1.0 / TOP)


def decode(coded, scale):
    return coded.astype(jnp.int32).astype(jnp.float32) * scale


def product(left, right):
    return lax.dot_general(
        left, right, (((1,), (1,)), ((), ())), preferred_element_type=jnp.float32
    )


def kernel(
    op_ref, em_ref, kt_ref, map_ref, counts_ref, out_ref,
    a_own, a_mate, b_own, b_mate, tiles, tm_ref, ac_ref,
    y_out, y_out_scale, y_in, y_in_scale,
    z_out, z_out_scale, z_in, z_in_scale, total,
    f_out, f_out_scale, f_in, f_in_scale, f_own, c_out, c_out_scale, c_in, c_in_scale,
    own_sem, table_sem, a_send, a_recv, b_send, b_recv, y_send, y_recv, z_send, z_recv,
    f_send, f_recv, c_send, c_recv,
):
    lines, cells = em_ref.shape[0], em_ref.shape[1]
    levels, rows = op_ref.shape[1], op_ref.shape[4]
    tile = kt_ref.shape[2]
    steps = total.shape[0]
    depth = steps // lines
    me = lax.axis_index("band")
    core = lax.rem(me, 2)
    y = lax.rem(me // 2, 2)
    z = me // 4
    mate = z * 4 + y * 2 + (1 - core)
    across = z * 4 + (1 - y) * 2 + core
    z_of = [lax.rem(z + d, levels) for d in range(levels)]
    along = [z_of[d] * 4 + y * 2 + core for d in range(levels)]

    def place(step):
        l = step // depth
        return l, pl.multiple_of((step - l * depth) * WIDTH, WIDTH)

    own_copies = [
        pltpu.make_async_copy(op_ref.at[l, :, side, core], a_own.at[l, side], own_sem.at[l, side])
        for l in range(lines)
        for side in range(2)
    ] + [pltpu.make_async_copy(em_ref.at[l], b_own.at[l], own_sem.at[l, 2]) for l in range(lines)]
    table_copies = [
        pltpu.make_async_copy(
            kt_ref.at[:, pl.ds(pl.multiple_of(core * rows, rows), rows), :], tiles, table_sem.at[0]
        ),
        pltpu.make_async_copy(map_ref, tm_ref, table_sem.at[1]),
        pltpu.make_async_copy(counts_ref, ac_ref, table_sem.at[2]),
    ]

    barrier = pltpu.get_barrier_semaphore()
    peers = [mate, across] + along[1:]
    for peer in peers:
        pl.semaphore_signal(barrier, inc=1, device_id={"band": peer}, device_id_type=MESH)
    for copy in own_copies + table_copies:
        copy.start()
    pl.semaphore_wait(barrier, len(peers))

    def a_copy(l, side):
        return pltpu.make_async_remote_copy(
            op_ref.at[l, :, side, 1 - core], a_mate.at[l, side],
            a_send.at[l, side], a_recv.at[l, side],
            device_id={"band": mate}, device_id_type=MESH,
        )

    def b_copy(step):
        l, column = place(step)
        span = pl.ds(column, WIDTH)
        return pltpu.make_async_remote_copy(
            em_ref.at[l, span, :], b_mate.at[l, span, :], b_send.at[step], b_recv.at[step],
            device_id={"band": mate}, device_id_type=MESH,
        )

    def y_copies(step):
        return (
            pltpu.make_async_remote_copy(
                y_out.at[step], y_in.at[step], y_send.at[step, 0], y_recv.at[step, 0],
                device_id={"band": across}, device_id_type=MESH,
            ),
            pltpu.make_async_remote_copy(
                y_out_scale.at[step], y_in_scale.at[step], y_send.at[step, 1], y_recv.at[step, 1],
                device_id={"band": across}, device_id_type=MESH,
            ),
        )

    def z_copies(step, d):
        return (
            pltpu.make_async_remote_copy(
                z_out.at[step, d - 1], z_in.at[step, d - 1],
                z_send.at[step, d - 1, 0], z_recv.at[step, d - 1, 0],
                device_id={"band": along[d]}, device_id_type=MESH,
            ),
            pltpu.make_async_remote_copy(
                z_out_scale.at[step, d - 1], z_in_scale.at[step, d - 1],
                z_send.at[step, d - 1, 1], z_recv.at[step, d - 1, 1],
                device_id={"band": along[d]}, device_id_type=MESH,
            ),
        )

    def f_copies(d):
        return (
            pltpu.make_async_remote_copy(
                f_out.at[d - 1], f_in.at[d - 1], f_send.at[d - 1, 0], f_recv.at[d - 1, 0],
                device_id={"band": along[d]}, device_id_type=MESH,
            ),
            pltpu.make_async_remote_copy(
                f_out_scale.at[d - 1], f_in_scale.at[d - 1],
                f_send.at[d - 1, 1], f_recv.at[d - 1, 1],
                device_id={"band": along[d]}, device_id_type=MESH,
            ),
        )

    c_copies = (
        pltpu.make_async_remote_copy(
            c_out, c_in, c_send.at[0], c_recv.at[0],
            device_id={"band": across}, device_id_type=MESH,
        ),
        pltpu.make_async_remote_copy(
            c_out_scale, c_in_scale, c_send.at[1], c_recv.at[1],
            device_id={"band": across}, device_id_type=MESH,
        ),
    )

    for l in range(lines):
        a_copy(l, 1 - y).start()
        b_copy(l * depth).start()
        if l == 0:
            b_copy(1).start()
            a_copy(l, y).start()

        @pl.loop(2 if l == 0 else 1, depth)
        def _(part):
            b_copy(l * depth + part).start()

        if l > 0:
            a_copy(l, y).start()

    for copy in own_copies + table_copies:
        copy.wait()

    def partial_sum(step, side):
        l, column = place(step)
        left_own = jnp.concatenate([a_own[l, side, z_of[d]] for d in range(levels)], axis=0)
        left_mate = jnp.concatenate([a_mate[l, side, z_of[d]] for d in range(levels)], axis=0)
        span = pl.ds(column, WIDTH)
        return product(left_own, b_own[l, span, :]) + product(left_mate, b_mate[l, span, :])

    def send_across(step):
        l, column = place(step)

        @pl.when((column == 0) & (l > 0))
        def _():
            a_copy(l, 1 - y).wait()

        b_copy(step).wait()
        sums = partial_sum(step, 1 - y)
        for d in range(levels):
            coded, scale = encode(sums[d * rows : (d + 1) * rows])
            y_out[step, d] = coded
            y_out_scale[step, d : d + 1] = scale
        for copy in y_copies(step):
            copy.start()

    def send_along(step):
        l, column = place(step)

        @pl.when((column == 0) & (l > 0))
        def _():
            a_copy(l, y).wait()

        sums = partial_sum(step, y)
        for copy in y_copies(step):
            copy.wait()
        for d in FAR_FIRST:
            block = sums[d * rows : (d + 1) * rows] + decode(
                y_in[step, d], y_in_scale[step, d : d + 1]
            )
            if d == 0:
                total[step] = block
            else:
                coded, scale = encode(block)
                z_out[step, d - 1] = coded
                z_out_scale[step, d - 1] = scale
                for copy in z_copies(step, d):
                    copy.start()

    row = lax.broadcasted_iota(jnp.int32, (rows, tile), 0) + me * rows
    lane = lax.broadcasted_iota(jnp.int32, (rows, tile), 1)

    def emit(step, block):
        l, first = place(step)
        live = ac_ref[l]
        for s in range(WIDTH // tile):
            coupling = block[:, s * tile : (s + 1) * tile]
            weight = tiles[tm_ref[l, me // 2, first // tile + s]]
            column = lane + (first + s * tile)
            result = weight * coupling
            result = jnp.where(row == column, result - 2.0 * coupling, result)
            inside = (row < live) & (column < live)
            start = pl.multiple_of(l * cells + first + s * tile, tile)
            out_ref[:, pl.ds(start, tile)] = jnp.where(inside, result, 0.0)

    def finish(step):
        block = total[step]
        for d in range(1, levels):
            for copy in z_copies(step, d):
                copy.wait()
            block = block + decode(z_in[step, d - 1], z_in_scale[step, d - 1])
        emit(step, block)

    def first_along():
        a_copy(0, y).wait()
        b_copy(0).wait()
        for side in range(2):
            sums = partial_sum(0, side)
            f_own[side] = sums[:rows]
            for d in range(1, levels):
                coded, scale = encode(sums[d * rows : (d + 1) * rows])
                f_out[d - 1, side] = coded
                f_out_scale[d - 1, side] = scale
        for d in FAR_FIRST[:-1]:
            for copy in f_copies(d):
                copy.start()

    def first_sum(side):
        block = f_own[side]
        for d in range(1, levels):
            block = block + decode(f_in[d - 1, side], f_in_scale[d - 1, side])
        return block

    def first_across():
        for d in range(1, levels):
            for copy in f_copies(d):
                copy.wait()
        coded, scale = encode(first_sum(1 - y))
        c_out[...] = coded
        c_out_scale[...] = scale
        for copy in c_copies:
            copy.start()

    a_copy(0, 1 - y).wait()
    first_along()
    send_across(1)
    send_across(2)

    @pl.loop(3, steps + LAG_ALONG + LAG_FINISH)
    def _(turn):
        @pl.when(turn < steps)
        def _():
            send_across(turn)

        @pl.when((turn > LAG_ALONG) & (turn < steps + LAG_ALONG))
        def _():
            send_along(turn - LAG_ALONG)

        @pl.when(turn == FIRST_ACROSS)
        def _():
            first_across()

        @pl.when(turn > LAG_ALONG + LAG_FINISH)
        def _():
            finish(turn - (LAG_ALONG + LAG_FINISH))

        @pl.when(turn == steps)
        def _():
            for copy in c_copies:
                copy.wait()
            emit(0, first_sum(y) + decode(c_in[...], c_in_scale[...]))


def fused_body(opacity_deriv, emission_deriv, kernel_tiles, tile_map, active_counts):
    lines, cells, bands = opacity_deriv.shape
    kinds, tile, _ = kernel_tiles.shape
    shards = lax.axis_size("band")
    rows = cells // shards
    levels = shards // 4
    steps = lines * (cells // WIDTH)
    vmem = pltpu.VMEM
    dma = pltpu.SemaphoreType.DMA
    half = jnp.bfloat16
    wide = jnp.float32
    out = pl.pallas_call(
        kernel,
        out_shape=pltpu.VMEM((rows, lines * cells), wide),
        in_specs=[pl.BlockSpec(memory_space=pltpu.HBM)] * 5,
        out_specs=pl.BlockSpec(memory_space=pltpu.VMEM),
        scratch_shapes=[
            vmem((lines, 2, levels, rows, bands), half),
            vmem((lines, 2, levels, rows, bands), half),
            vmem((lines, cells, bands), half),
            vmem((lines, cells, bands), half),
            vmem((kinds, rows, tile), wide),
            pltpu.SMEM(tile_map.shape, tile_map.dtype),
            pltpu.SMEM(active_counts.shape, active_counts.dtype),
            vmem((steps, levels, rows, WIDTH), jnp.int16),
            vmem((steps, levels, WIDTH), wide),
            vmem((steps, levels, rows, WIDTH), jnp.int16),
            vmem((steps, levels, WIDTH), wide),
            vmem((steps, levels - 1, rows, WIDTH), jnp.int16),
            vmem((steps, levels - 1, 1, WIDTH), wide),
            vmem((steps, levels - 1, rows, WIDTH), jnp.int16),
            vmem((steps, levels - 1, 1, WIDTH), wide),
            vmem((steps, rows, WIDTH), wide),
            vmem((levels - 1, 2, rows, WIDTH), jnp.int16),
            vmem((levels - 1, 2, 1, WIDTH), wide),
            vmem((levels - 1, 2, rows, WIDTH), jnp.int16),
            vmem((levels - 1, 2, 1, WIDTH), wide),
            vmem((2, rows, WIDTH), wide),
            vmem((rows, WIDTH), jnp.int16),
            vmem((1, WIDTH), wide),
            vmem((rows, WIDTH), jnp.int16),
            vmem((1, WIDTH), wide),
            dma((lines, 3)),
            dma((3,)),
            dma((lines, 2)),
            dma((lines, 2)),
            dma((steps,)),
            dma((steps,)),
            dma((steps, 2)),
            dma((steps, 2)),
            dma((steps, levels - 1, 2)),
            dma((steps, levels - 1, 2)),
            dma((levels - 1, 2)),
            dma((levels - 1, 2)),
            dma((2,)),
            dma((2,)),
        ],
        compiler_params=pltpu.CompilerParams(
            collective_id=0, has_side_effects=True, vmem_limit_bytes=62 * 1024 * 1024
        ),
        cost_estimate=pl.CostEstimate(
            flops=2 * lines * cells * cells * bands,
            bytes_accessed=4 * lines * cells * bands,
            transcendentals=0,
        ),
        name="band_sum",
    )(
        opacity_deriv.reshape(lines, levels, 2, 2, rows, bands),
        emission_deriv,
        kernel_tiles,
        tile_map,
        active_counts,
    )
    return out.reshape(rows, lines, cells)


def solution(mesh):
    body = fused_body if mesh.shape["band"] == 16 else plain_body
    return jax.shard_map(
        body,
        mesh=mesh,
        in_specs=(
            P("grp", None, "band"),
            P("grp", None, "band"),
            P(),
            P("grp", None, None),
            P("grp"),
        ),
        out_specs=P("band", "grp", None),
        check_vma=False,
    )
```
